32 devices in a mesh: groups: 2 (over y), blk: 8 (over z, x), dim: 2 (over core).
Axes of the slice: x: 2, y: 2, z: 4, core: 2. Of those that a mesh axis runs over, the one named last changes fastest.
Arguments:
- queries: bfloat16 [128, 8192], P('blk', 'dim'), may hold values from -6 to 6
- train_proj: bfloat16 [6144, 8192], P(('groups', 'blk'), 'dim'), parts along dimension 0, may hold values from -6 to 6
- basis: bfloat16 [64, 128, 128], P('dim'), may hold values from -0.5 to 0.5
- inv_eigen: float32 [64, 128], P('dim'), may hold values from 0.1 to 3
Outputs:
- scores: float32 [128, 6144], P(None, ('groups', 'blk', 'dim')), parts along dimension 1
The draws below stay inside these ranges and needn't reach their ends.
There are 2 independent parts, one for each index of `groups`. The reference program is written for one: setup_inputs(seed, part) draws one part's arguments, and reference() takes and returns one part's arrays. A program takes and returns all parts, laid end to end along the dimension named above; an argument that names none is the same for every part. Nothing has to cross between parts.
All inputs are finite; a program needn't handle non-finite values.
Results may differ from the reference program's by a relative error of at most 0.0037.
Values may be sent and summed in bfloat16 or wider, within the bound.
A program may use at most 64 MiB of HBM per device.

```python
import math
import jax
import jax.numpy as jnp
from jax import lax

MODULES = 64
BSZ = 128
PROJ = 8192
Q_TOTAL = 128
TRAIN = 3072


def level_of(key, shape, cuts, least, high):
    def one(dim, parts):
        heights = jax.random.uniform(jax.random.fold_in(jax.random.fold_in(key, 6), dim), (parts,), jnp.float32, least / len(cuts), high / len(cuts))
        return jnp.repeat(jnp.exp(heights), shape[dim] // parts).reshape((-1,) + (1,) * (len(shape) - dim - 1))

    level = one(*cuts[0])
    for cut in cuts[1:]:
        level = level * one(*cut)
    return level


def normal_values(own_key, dims, width, reach, cuts=(), dtype=jnp.bfloat16):
    array = width * jax.random.normal(own_key, dims, jnp.float32)
    if cuts:
        array = array * level_of(own_key, dims, cuts, -0.22, 0.18)
    return jnp.clip(array, -reach, reach).astype(dtype)


def setup_inputs(seed: int = 0, part: int = 0) -> dict:
    key_of = jax.random.split(jax.random.key(seed), 5)
    part_keys = jax.random.split(jax.random.fold_in(key_of[4], part), 5)
    return {
        "queries": normal_values(key_of[0], (Q_TOTAL, PROJ), 1.0, 6.0, ((0, 8), (1, 2))),
        "train_proj": normal_values(part_keys[1], (TRAIN, PROJ), 1.0, 6.0, ((0, 8), (1, 2))),
        "basis": normal_values(key_of[2], (MODULES, BSZ, BSZ), BSZ ** -0.5, 0.5, ((0, 2),)),
        "inv_eigen": jnp.clip(jnp.exp(math.log(3.0) - 3.4011974 * jax.random.uniform(key_of[3], (MODULES, BSZ), jnp.float32) ** level_of(key_of[3], (MODULES, BSZ), ((0, 2),), -0.2, 0.2)), 0.1, 3.0),
    }


def reference(queries, train_proj, basis, inv_eigen):
    count = queries.shape[0]
    blocks = queries.reshape(count, MODULES, BSZ).astype(jnp.float32)
    basis_f = basis.astype(jnp.float32)
    rotated = jnp.einsum('qmb,mbc->qmc', blocks, basis_f) * inv_eigen[None, :, :]
    rotated = rotated.astype(jnp.bfloat16).astype(jnp.float32)
    precond = jnp.einsum('qmc,mbc->qmb', rotated, basis_f).astype(jnp.bfloat16)
    precond = precond.reshape(count, PROJ)
    total = lax.dot_general(precond, train_proj, (((1,), (1,)), ((), ())), preferred_element_type=jnp.float32)
    return total / jnp.sqrt(jnp.float32(PROJ))
```

```python
import functools

import jax
import jax.numpy as jnp
from jax import lax
from jax.experimental import pallas as pl
from jax.experimental.pallas import tpu as pltpu
from jax.sharding import PartitionSpec as P

PROJ = 8192
MESH = pl.DeviceIdType.MESH
X = 2
Z = 4
SPLIT = 1536


def order(z, s):
    near = jnp.minimum(z, Z - 1 - z)
    both = s <= 2 * near
    side = jnp.where(both, 2 * (s % 2) - 1, jnp.where(2 * z < Z, 1, -1))
    dist = jnp.where(both, (s + 1) // 2, s - near)
    return z + side * dist, side


def kernel(q_hbm, train_hbm, basis_hbm, inv_hbm, out, buf, train, basis, inv, pq, keep, give, got,
           load_sem, send_sem, recv_sem, give_sem, got_sem):
    rows, width = q_hbm.shape
    half = train_hbm.shape[0] // 2
    modules, bsz, _ = basis_hbm.shape
    y, b, d = lax.axis_index("groups"), lax.axis_index("blk"), lax.axis_index("dim")
    z, x = b // X, b % X

    loads = [pltpu.make_async_copy(basis_hbm, basis, load_sem.at[0]),
             pltpu.make_async_copy(inv_hbm, inv, load_sem.at[1]),
             pltpu.make_async_copy(q_hbm, buf.at[z, pl.ds(pl.multiple_of(x * rows, rows), rows)], load_sem.at[2])]
    for i in range(2):
        at = pl.multiple_of((d if i == 0 else 1 - d) * half, 16)
        loads.append(pltpu.make_async_copy(train_hbm.at[pl.ds(at, half)], train.at[i], load_sem.at[3 + i]))
    for load in loads:
        load.start()

    up, down = z + 1 < Z, z > 0
    barrier = pltpu.get_barrier_semaphore()

    def hello(**device):
        pl.semaphore_signal(barrier, inc=1, device_id=device, device_id_type=MESH)

    hello(blk=z * X + 1 - x)
    hello(groups=1 - y)
    hello(dim=1 - d)

    @pl.when(up)
    def _():
        hello(blk=b + X)

    @pl.when(down)
    def _():
        hello(blk=b - X)

    pl.semaphore_wait(barrier, 3 + jnp.where(up, 1, 0) + jnp.where(down, 1, 0))

    mine = (0, pl.multiple_of(y * SPLIT, 128), SPLIT)
    other = (1, pl.multiple_of((1 - y) * SPLIT, 128), SPLIT)
    common = (2, 2 * SPLIT, width - 2 * SPLIT)
    carried = (mine, common)
    sends = []

    def place(oz, ox, part):
        return buf.at[oz, pl.ds(pl.multiple_of(ox * rows, rows), rows), pl.ds(part[1], part[2])]

    def send(cond, oz, ox, part, device, own=False):
        name = 2 if part[0] == 2 else (y if part[0] == 0 else 1 - y)
        src = q_hbm.at[:, pl.ds(part[1], part[2])] if own else place(oz, ox, part)
        copy = pltpu.make_async_remote_copy(
            src_ref=src, dst_ref=place(oz, ox, part),
            send_sem=send_sem.at[len(sends)], recv_sem=recv_sem.at[oz * X + ox, name],
            device_id=device, device_id_type=MESH)
        sends.append((cond, copy))
        if cond is None:
            copy.start()
        else:
            pl.when(cond)(copy.start)

    def arrive(oz, ox, part):
        name = 2 if part[0] == 2 else (y if part[0] == 0 else 1 - y)
        here = place(oz, ox, part)
        pltpu.make_async_copy(here, here, recv_sem.at[oz * X + ox, name]).wait()

    for part in carried:
        send(up, z, x, part, {"blk": b + X}, own=True)
        send(down, z, x, part, {"blk": b - X}, own=True)
        send(None, z, x, part, {"blk": z * X + 1 - x}, own=True)

    loads[2].wait()
    gives = []
    for s in range(Z):
        if s + 1 < Z:
            oz, side = order(z, s + 1)
            onward = (z - side >= 0) & (z - side < Z)
            for part in carried:
                arrive(oz, x, part)
                send(onward, oz, x, part, {"blk": b - side * X})
                send(None, oz, x, part, {"blk": z * X + 1 - x})
                if part[0] == 0:
                    send(None, oz, x, part, {"groups": 1 - y})
        oz, _ = order(z, s) if s else (z, None)
        for part in carried:
            arrive(oz, 1 - x, part)
            if part[0] == 0:
                send(None, oz, 1 - x, part, {"groups": 1 - y})
        if s:
            arrive(oz, x, other)
        arrive(oz, 1 - x, other)
        if s == 0:
            loads[0].wait()
            loads[1].wait()
        for m in range(modules):
            cols = slice(m * bsz, (m + 1) * bsz)
            rot = jnp.dot(buf[oz, :, cols], basis[m], preferred_element_type=jnp.float32) * inv[m:m + 1, :]
            pre = lax.dot_general(rot.astype(jnp.bfloat16), basis[m], (((1,), (1,)), ((), ())),
                                  preferred_element_type=jnp.float32)
            pq[:, cols] = pre.astype(jnp.bfloat16)
        if s == 0:
            loads[3].wait()
            loads[4].wait()
        there = pl.ds(pl.multiple_of(oz * X * rows, X * rows), X * rows)
        give[there, :] = lax.dot_general(pq[...], train[1], (((1,), (1,)), ((), ())),
                                         preferred_element_type=jnp.float32)
        copy = pltpu.make_async_remote_copy(
            src_ref=give.at[there], dst_ref=got.at[there], send_sem=give_sem.at[s], recv_sem=got_sem.at[s],
            device_id={"dim": 1 - d}, device_id_type=MESH)
        copy.start()
        gives.append((copy, there))
        keep[there, :] = lax.dot_general(pq[...], train[0], (((1,), (1,)), ((), ())),
                                         preferred_element_type=jnp.float32)

    factor = 1.0 / (PROJ ** 0.5)
    for copy, there in gives:
        copy.wait_recv()
        out[there, :] = (keep[there, :] + got[there, :]) * factor
    for cond, copy in sends:
        if cond is None:
            copy.wait_send()
        else:
            pl.when(cond)(copy.wait_send)
    for copy, _ in gives:
        copy.wait_send()


def fused(queries, train_proj, basis, inv_eigen):
    rows, width = queries.shape
    examples = train_proj.shape[0]
    total = rows * X * Z
    half = (total, examples // 2)
    hbm = pl.BlockSpec(memory_space=pl.ANY)
    vmem = pl.BlockSpec(memory_space=pltpu.VMEM)
    return pl.pallas_call(
        kernel,
        out_shape=jax.ShapeDtypeStruct(half, jnp.float32),
        in_specs=[hbm] * 4,
        out_specs=vmem,
        scratch_shapes=[
            pltpu.VMEM((Z, X * rows, width), jnp.bfloat16),
            pltpu.VMEM((2, examples // 2, width), jnp.bfloat16),
            pltpu.VMEM(basis.shape, basis.dtype),
            pltpu.VMEM(inv_eigen.shape, inv_eigen.dtype),
            pltpu.VMEM((X * rows, width), jnp.bfloat16),
            pltpu.VMEM(half, jnp.float32),
            pltpu.VMEM(half, jnp.float32),
            pltpu.VMEM(half, jnp.float32),
            pltpu.SemaphoreType.DMA((5,)),
            pltpu.SemaphoreType.DMA((40,)),
            pltpu.SemaphoreType.DMA((X * Z, 3)),
            pltpu.SemaphoreType.DMA((Z,)),
            pltpu.SemaphoreType.DMA((Z,)),
        ],
        compiler_params=pltpu.CompilerParams(
            collective_id=0, has_side_effects=True, vmem_limit_bytes=48 * 1024 * 1024),
        cost_estimate=pl.CostEstimate(flops=2 * total * width * (examples + 256), transcendentals=0,
                                      bytes_accessed=2 * width * (examples + 256)),
    )(queries, train_proj, basis, inv_eigen)


def precondition(queries, basis, inv_eigen):
    count = queries.shape[0]
    local_modules = basis.shape[0]
    width = basis.shape[1]
    blocks = queries.reshape(count, local_modules, width)
    rotated = (
        jnp.einsum("qmb,mbc->qmc", blocks, basis, preferred_element_type=jnp.float32)
        * inv_eigen[None, :, :]
    )
    rotated = rotated.astype(jnp.bfloat16)
    precond = jnp.einsum("qmc,mbc->qmb", rotated, basis, preferred_element_type=jnp.float32).astype(
        jnp.bfloat16
    )
    return precond.reshape(count, local_modules * width)


def shards(queries, train_proj, basis, inv_eigen):
    precond = precondition(queries, basis, inv_eigen)
    factor = 1.0 / jnp.sqrt(jnp.float32(PROJ))
    terms = lax.dot_general(
        lax.all_gather(precond, "blk", axis=0, tiled=True),
        train_proj,
        (((1,), (1,)), ((), ())),
        preferred_element_type=jnp.float32,
    )
    half = train_proj.shape[0] // lax.axis_size("dim")
    summed = lax.psum(terms, "dim")
    own = lax.dynamic_slice_in_dim(summed, lax.axis_index("dim") * half, half, 1)
    return own * factor


def solution(mesh):
    placed = (P("blk", "dim"), P(("groups", "blk"), "dim"), P("dim", None, None), P("dim", None))
    small = mesh.shape["blk"] == X * Z and mesh.shape["groups"] == 2 and mesh.shape["dim"] == 2
    return jax.shard_map(
        fused if small else shards,
        mesh=mesh,
        in_specs=placed,
        out_specs=P(None, ("groups", "blk", "dim")),
        check_vma=False,
    )
```

```python
import functools

import jax
import jax.numpy as jnp
from jax import lax
from jax.experimental import pallas as pl
from jax.experimental.pallas import tpu as pltpu
from jax.sharding import PartitionSpec as P

PROJ = 8192
MESH = pl.DeviceIdType.MESH
X = 2
Z = 4
SPLIT = 1536


def order(z, s):
    near = jnp.minimum(z, Z - 1 - z)
    both = s <= 2 * near
    side = jnp.where(both, 2 * (s % 2) - 1, jnp.where(2 * z < Z, 1, -1))
    dist = jnp.where(both, (s + 1) // 2, s - near)
    return z + side * dist, side


def kernel(q_hbm, train_hbm, basis_hbm, inv_hbm, out, q, rot, buf, train, basis, inv, keep, give, got,
           load_sem, send_sem, recv_sem, give_sem, got_sem):
    rows, width = q_hbm.shape
    half = train_hbm.shape[0] // 2
    bsz = basis_hbm.shape[1]
    y, b, d = lax.axis_index("groups"), lax.axis_index("blk"), lax.axis_index("dim")
    z, x = b // X, b % X
    planes = [order(z, s)[0] for s in range(1, Z)]

    barrier = pltpu.get_barrier_semaphore()

    def hello(**device):
        pl.semaphore_signal(barrier, inc=1, device_id=device, device_id_type=MESH)

    hello(blk=z * X + 1 - x)
    hello(groups=1 - y)
    hello(dim=1 - d)
    for oz in planes:
        hello(blk=oz * X + x)

    loads = [pltpu.make_async_copy(basis_hbm, basis, load_sem.at[0]),
             pltpu.make_async_copy(inv_hbm, inv, load_sem.at[1]),
             pltpu.make_async_copy(q_hbm, q, load_sem.at[2])]
    for i in range(2):
        at = pl.multiple_of((d if i == 0 else 1 - d) * half, 16)
        loads.append(pltpu.make_async_copy(train_hbm.at[pl.ds(at, half)], train.at[i], load_sem.at[3 + i]))
    for load in loads:
        load.start()

    mine = (y * SPLIT, SPLIT, y)
    other = ((1 - y) * SPLIT, SPLIT, 1 - y)
    common = (2 * SPLIT, width - 2 * SPLIT, 2)
    sends = []

    def columns(part):
        start = part[0] if isinstance(part[0], int) else pl.multiple_of(part[0], 128)
        return pl.ds(start, part[1])

    def lines(oz, ox):
        return pl.ds(pl.multiple_of((oz * X + ox) * rows, rows), rows)

    def send(oz, ox, part, device):
        place = buf.at[lines(oz, ox), columns(part)]
        copy = pltpu.make_async_remote_copy(
            src_ref=place, dst_ref=place,
            send_sem=send_sem.at[len(sends)], recv_sem=recv_sem.at[oz * X + ox, part[2]],
            device_id=device, device_id_type=MESH)
        copy.start()
        sends.append(copy)

    def arrive(oz, ox, part):
        place = buf.at[lines(oz, ox), columns(part)]
        pltpu.make_async_copy(place, place, recv_sem.at[oz * X + ox, part[2]]).wait()

    def precondition_own(part):
        for i in range(part[1] // bsz):
            m = part[0] // bsz + i
            cols = columns((part[0] + i * bsz, bsz))
            first = jnp.dot(q[:, cols], basis[m], preferred_element_type=jnp.float32)
            rot[:, i * bsz:(i + 1) * bsz] = (first * inv[pl.ds(m, 1), :]).astype(jnp.bfloat16)
        for i in range(part[1] // bsz):
            m = part[0] // bsz + i
            second = lax.dot_general(rot[:, i * bsz:(i + 1) * bsz], basis[m], (((1,), (1,)), ((), ())),
                                     preferred_element_type=jnp.float32)
            buf[lines(z, x), columns((part[0] + i * bsz, bsz))] = second.astype(jnp.bfloat16)

    for load in loads[:3]:
        load.wait()
    precondition_own(mine)
    pl.semaphore_wait(barrier, Z + 2)
    for part in (mine, common):
        if part is common:
            precondition_own(common)
        send(z, x, part, {"blk": z * X + 1 - x})
        for oz in planes:
            send(z, x, part, {"blk": oz * X + x})
    precondition_own(other)

    def hand_over(oz):
        for part in (mine, common):
            arrive(oz, 1 - x, part)
            if part is mine:
                send(oz, 1 - x, part, {"groups": 1 - y})

    hand_over_next = z
    for oz in planes:
        for part in (mine, common):
            arrive(oz, x, part)
            send(oz, x, part, {"blk": z * X + 1 - x})
            if part is mine:
                send(oz, x, part, {"groups": 1 - y})
        hand_over(hand_over_next)
        hand_over_next = oz
    hand_over(hand_over_next)

    def score(i, part):
        return lax.dot_general(buf[:, columns(part)], train[i, :, columns(part)], (((1,), (1,)), ((), ())),
                               preferred_element_type=jnp.float32)

    loads[3].wait()
    loads[4].wait()
    give[...] = score(1, mine) + score(1, common)
    keep[...] = score(0, mine) + score(0, common)
    arrive(z, 1 - x, other)
    for oz in planes:
        arrive(oz, x, other)
        arrive(oz, 1 - x, other)
    give[...] += score(1, other)
    swap = pltpu.make_async_remote_copy(src_ref=give, dst_ref=got, send_sem=give_sem, recv_sem=got_sem,
                                        device_id={"dim": 1 - d}, device_id_type=MESH)
    swap.start()
    keep[...] += score(0, other)
    swap.wait_recv()
    out[...] = (keep[...] + got[...]) * (1.0 / (PROJ ** 0.5))
    for copy in sends:
        copy.wait_send()
    swap.wait_send()


def fused(queries, train_proj, basis, inv_eigen):
    rows, width = queries.shape
    examples = train_proj.shape[0]
    total = rows * X * Z
    half = (total, examples // 2)
    hbm = pl.BlockSpec(memory_space=pl.ANY)
    vmem = pl.BlockSpec(memory_space=pltpu.VMEM)
    return pl.pallas_call(
        kernel,
        out_shape=jax.ShapeDtypeStruct(half, jnp.float32),
        in_specs=[hbm] * 4,
        out_specs=vmem,
        scratch_shapes=[
            pltpu.VMEM((rows, width), jnp.bfloat16),
            pltpu.VMEM((rows, width), jnp.bfloat16),
            pltpu.VMEM((total, width), jnp.bfloat16),
            pltpu.VMEM((2, examples // 2, width), jnp.bfloat16),
            pltpu.VMEM(basis.shape, basis.dtype),
            pltpu.VMEM(inv_eigen.shape, inv_eigen.dtype),
            pltpu.VMEM(half, jnp.float32),
            pltpu.VMEM(half, jnp.float32),
            pltpu.VMEM(half, jnp.float32),
            pltpu.SemaphoreType.DMA((5,)),
            pltpu.SemaphoreType.DMA((2 * Z + 3 * (Z - 1) + Z,)),
            pltpu.SemaphoreType.DMA((X * Z, 3)),
            pltpu.SemaphoreType.DMA,
            pltpu.SemaphoreType.DMA,
        ],
        compiler_params=pltpu.CompilerParams(
            collective_id=0, has_side_effects=True, vmem_limit_bytes=60 * 1024 * 1024),
        cost_estimate=pl.CostEstimate(flops=2 * total * width * (examples + 256), transcendentals=0,
                                      bytes_accessed=2 * width * (examples + 256)),
    )(queries, train_proj, basis, inv_eigen)


def precondition(queries, basis, inv_eigen):
    count = queries.shape[0]
    local_modules = basis.shape[0]
    width = basis.shape[1]
    blocks = queries.reshape(count, local_modules, width)
    rotated = (
        jnp.einsum("qmb,mbc->qmc", blocks, basis, preferred_element_type=jnp.float32)
        * inv_eigen[None, :, :]
    )
    rotated = rotated.astype(jnp.bfloat16)
    precond = jnp.einsum("qmc,mbc->qmb", rotated, basis, preferred_element_type=jnp.float32).astype(
        jnp.bfloat16
    )
    return precond.reshape(count, local_modules * width)


def shards(queries, train_proj, basis, inv_eigen):
    precond = precondition(queries, basis, inv_eigen)
    factor = 1.0 / jnp.sqrt(jnp.float32(PROJ))
    terms = lax.dot_general(
        lax.all_gather(precond, "blk", axis=0, tiled=True),
        train_proj,
        (((1,), (1,)), ((), ())),
        preferred_element_type=jnp.float32,
    )
    half = train_proj.shape[0] // lax.axis_size("dim")
    summed = lax.psum(terms, "dim")
    own = lax.dynamic_slice_in_dim(summed, lax.axis_index("dim") * half, half, 1)
    return own * factor


def solution(mesh):
    placed = (P("blk", "dim"), P(("groups", "blk"), "dim"), P("dim", None, None), P("dim", None))
    small = mesh.shape["blk"] == X * Z and mesh.shape["groups"] == 2 and mesh.shape["dim"] == 2
    return jax.shard_map(
        fused if small else shards,
        mesh=mesh,
        in_specs=placed,
        out_specs=P(None, ("groups", "blk", "dim")),
        check_vma=False,
    )
```

```python
import functools

import jax
import jax.numpy as jnp
from jax import lax
from jax.experimental import pallas as pl
from jax.experimental.pallas import tpu as pltpu
from jax.sharding import PartitionSpec as P

PROJ = 8192
MESH = pl.DeviceIdType.MESH
X = 2
Z = 4


def order(z, s):
    near = jnp.minimum(z, Z - 1 - z)
    both = s <= 2 * near
    side = jnp.where(both, 2 * (s % 2) - 1, jnp.where(2 * z < Z, 1, -1))
    dist = jnp.where(both, (s + 1) // 2, s - near)
    return z + side * dist, side


def kernel(q_hbm, train_hbm, basis_hbm, inv_hbm, out, q, rot, buf, train, basis, inv, keep, give, got,
           load_sem, send_sem, recv_sem, give_sem, got_sem):
    rows, width = q_hbm.shape
    half = train_hbm.shape[0] // 2
    bsz = basis_hbm.shape[1]
    y, b, d = lax.axis_index("groups"), lax.axis_index("blk"), lax.axis_index("dim")
    z, x = b // X, b % X
    planes = [order(z, s)[0] for s in range(1, Z)]

    barrier = pltpu.get_barrier_semaphore()

    def hello(**device):
        pl.semaphore_signal(barrier, inc=1, device_id=device, device_id_type=MESH)

    hello(blk=z * X + 1 - x)
    hello(groups=1 - y)
    hello(dim=1 - d)
    for oz in planes:
        hello(blk=oz * X + x)

    loads = [pltpu.make_async_copy(basis_hbm, basis, load_sem.at[0]),
             pltpu.make_async_copy(inv_hbm, inv, load_sem.at[1]),
             pltpu.make_async_copy(q_hbm, q, load_sem.at[2])]
    for i in range(2):
        at = pl.multiple_of((d if i == 0 else 1 - d) * half, 16)
        loads.append(pltpu.make_async_copy(train_hbm.at[pl.ds(at, half)], train.at[i], load_sem.at[3 + i]))
    for load in loads:
        load.start()

    split = width // 2
    mine = (y * split, split, y)
    other = ((1 - y) * split, split, 1 - y)
    whole = (0, width, 2)
    sends = []

    def columns(part):
        start = part[0] if isinstance(part[0], int) else pl.multiple_of(part[0], 128)
        return pl.ds(start, part[1])

    def lines(oz, ox):
        return pl.ds(pl.multiple_of((oz * X + ox) * rows, rows), rows)

    def send(oz, ox, part, device):
        place = buf.at[lines(oz, ox), columns(part)]
        copy = pltpu.make_async_remote_copy(
            src_ref=place, dst_ref=place,
            send_sem=send_sem.at[len(sends)], recv_sem=recv_sem.at[oz * X + ox, part[2]],
            device_id=device, device_id_type=MESH)
        copy.start()
        sends.append(copy)

    def arrive(oz, ox, part):
        place = buf.at[lines(oz, ox), columns(part)]
        pltpu.make_async_copy(place, place, recv_sem.at[oz * X + ox, part[2]]).wait()

    def precondition_own(part):
        for i in range(part[1] // bsz):
            m = part[0] // bsz + i
            cols = columns((part[0] + i * bsz, bsz))
            first = jnp.dot(q[:, cols], basis[m], preferred_element_type=jnp.float32)
            rot[:, i * bsz:(i + 1) * bsz] = (first * inv[pl.ds(m, 1), :]).astype(jnp.bfloat16)
        for i in range(part[1] // bsz):
            m = part[0] // bsz + i
            second = lax.dot_general(rot[:, i * bsz:(i + 1) * bsz], basis[m], (((1,), (1,)), ((), ())),
                                     preferred_element_type=jnp.float32)
            buf[lines(z, x), columns((part[0] + i * bsz, bsz))] = second.astype(jnp.bfloat16)

    for load in loads[:3]:
        load.wait()
    precondition_own(mine)
    pl.semaphore_wait(barrier, Z + 2)
    for oz in planes:
        send(z, x, mine, {"blk": oz * X + x})
    precondition_own(other)
    send(z, x, whole, {"blk": z * X + 1 - x})

    def hand_over(oz):
        arrive(oz, 1 - x, mine)
        send(oz, 1 - x, mine, {"groups": 1 - y})

    for s, oz in enumerate(planes):
        arrive(oz, x, mine)
        send(oz, x, mine, {"groups": 1 - y})
        send(oz, x, mine, {"blk": z * X + 1 - x})
        if s:
            hand_over(planes[s - 1])
    hand_over(planes[-1])
    arrive(z, 1 - x, whole)

    def score(i, part):
        return lax.dot_general(buf[:, columns(part)], train[i, :, columns(part)], (((1,), (1,)), ((), ())),
                               preferred_element_type=jnp.float32)

    loads[3].wait()
    loads[4].wait()
    give[...] = score(1, mine)
    keep[...] = score(0, mine)
    for oz in planes:
        arrive(oz, x, other)
        arrive(oz, 1 - x, other)
    give[...] += score(1, other)
    swap = pltpu.make_async_remote_copy(src_ref=give, dst_ref=got, send_sem=give_sem, recv_sem=got_sem,
                                        device_id={"dim": 1 - d}, device_id_type=MESH)
    swap.start()
    keep[...] += score(0, other)
    swap.wait_recv()
    out[...] = (keep[...] + got[...]) * (1.0 / (PROJ ** 0.5))
    for copy in sends:
        copy.wait_send()
    swap.wait_send()


def fused(queries, train_proj, basis, inv_eigen):
    rows, width = queries.shape
    examples = train_proj.shape[0]
    total = rows * X * Z
    half = (total, examples // 2)
    hbm = pl.BlockSpec(memory_space=pl.ANY)
    vmem = pl.BlockSpec(memory_space=pltpu.VMEM)
    return pl.pallas_call(
        kernel,
        out_shape=jax.ShapeDtypeStruct(half, jnp.float32),
        in_specs=[hbm] * 4,
        out_specs=vmem,
        scratch_shapes=[
            pltpu.VMEM((rows, width), jnp.bfloat16),
            pltpu.VMEM((rows, width), jnp.bfloat16),
            pltpu.VMEM((total, width), jnp.bfloat16),
            pltpu.VMEM((2, examples // 2, width), jnp.bfloat16),
            pltpu.VMEM(basis.shape, basis.dtype),
            pltpu.VMEM(inv_eigen.shape, inv_eigen.dtype),
            pltpu.VMEM(half, jnp.float32),
            pltpu.VMEM(half, jnp.float32),
            pltpu.VMEM(half, jnp.float32),
            pltpu.SemaphoreType.DMA((5,)),
            pltpu.SemaphoreType.DMA((4 * Z,)),
            pltpu.SemaphoreType.DMA((X * Z, 3)),
            pltpu.SemaphoreType.DMA,
            pltpu.SemaphoreType.DMA,
        ],
        compiler_params=pltpu.CompilerParams(
            collective_id=0, has_side_effects=True, vmem_limit_bytes=60 * 1024 * 1024),
        cost_estimate=pl.CostEstimate(flops=2 * total * width * (examples + 256), transcendentals=0,
                                      bytes_accessed=2 * width * (examples + 256)),
    )(queries, train_proj, basis, inv_eigen)


def precondition(queries, basis, inv_eigen):
    count = queries.shape[0]
    local_modules = basis.shape[0]
    width = basis.shape[1]
    blocks = queries.reshape(count, local_modules, width)
    rotated = (
        jnp.einsum("qmb,mbc->qmc", blocks, basis, preferred_element_type=jnp.float32)
        * inv_eigen[None, :, :]
    )
    rotated = rotated.astype(jnp.bfloat16)
    precond = jnp.einsum("qmc,mbc->qmb", rotated, basis, preferred_element_type=jnp.float32).astype(
        jnp.bfloat16
    )
    return precond.reshape(count, local_modules * width)


def shards(queries, train_proj, basis, inv_eigen):
    precond = precondition(queries, basis, inv_eigen)
    factor = 1.0 / jnp.sqrt(jnp.float32(PROJ))
    terms = lax.dot_general(
        lax.all_gather(precond, "blk", axis=0, tiled=True),
        train_proj,
        (((1,), (1,)), ((), ())),
        preferred_element_type=jnp.float32,
    )
    half = train_proj.shape[0] // lax.axis_size("dim")
    summed = lax.psum(terms, "dim")
    own = lax.dynamic_slice_in_dim(summed, lax.axis_index("dim") * half, half, 1)
    return own * factor


def solution(mesh):
    placed = (P("blk", "dim"), P(("groups", "blk"), "dim"), P("dim", None, None), P("dim", None))
    small = mesh.shape["blk"] == X * Z and mesh.shape["groups"] == 2 and mesh.shape["dim"] == 2
    return jax.shard_map(
        fused if small else shards,
        mesh=mesh,
        in_specs=placed,
        out_specs=P(None, ("groups", "blk", "dim")),
        check_vma=False,
    )
```

```python
import functools

import jax
import jax.numpy as jnp
from jax import lax
from jax.experimental import pallas as pl
from jax.experimental.pallas import tpu as pltpu
from jax.sharding import PartitionSpec as P

PROJ = 8192
MESH = pl.DeviceIdType.MESH
X = 2
Z = 4


def order(z, s):
    near = jnp.minimum(z, Z - 1 - z)
    both = s <= 2 * near
    side = jnp.where(both, 2 * (s % 2) - 1, jnp.where(2 * z < Z, 1, -1))
    dist = jnp.where(both, (s + 1) // 2, s - near)
    return z + side * dist, side


def kernel(q_hbm, train_hbm, basis_hbm, inv_hbm, out, q, rot, buf, train, basis, inv, keep, give, got,
           load_sem, send_sem, recv_sem, give_sem, got_sem):
    rows, width = q_hbm.shape
    half = train_hbm.shape[0] // 2
    bsz = basis_hbm.shape[1]
    y, b, d = lax.axis_index("groups"), lax.axis_index("blk"), lax.axis_index("dim")
    z, x = b // X, b % X
    planes = [order(z, s)[0] for s in range(1, Z)]

    barrier = pltpu.get_barrier_semaphore()

    def hello(**device):
        pl.semaphore_signal(barrier, inc=1, device_id=device, device_id_type=MESH)

    hello(blk=z * X + 1 - x)
    hello(groups=1 - y)
    hello(dim=1 - d)
    for oz in planes:
        hello(blk=oz * X + x)

    loads = [pltpu.make_async_copy(basis_hbm, basis, load_sem.at[0]),
             pltpu.make_async_copy(inv_hbm, inv, load_sem.at[1]),
             pltpu.make_async_copy(q_hbm, q, load_sem.at[2])]
    for i in range(2):
        at = pl.multiple_of((d if i == 0 else 1 - d) * half, 16)
        loads.append(pltpu.make_async_copy(train_hbm.at[pl.ds(at, half)], train.at[i], load_sem.at[3 + i]))
    for load in loads:
        load.start()

    split = width // 2
    mine = (y * split, split, y)
    other = ((1 - y) * split, split, 1 - y)
    whole = (0, width, 2)
    sends = []

    def columns(part):
        start = part[0] if isinstance(part[0], int) else pl.multiple_of(part[0], 128)
        return pl.ds(start, part[1])

    def lines(oz, ox):
        return pl.ds(pl.multiple_of((oz * X + ox) * rows, rows), rows)

    def send(oz, ox, part, device):
        place = buf.at[lines(oz, ox), columns(part)]
        copy = pltpu.make_async_remote_copy(
            src_ref=place, dst_ref=place,
            send_sem=send_sem.at[len(sends)], recv_sem=recv_sem.at[oz * X + ox, part[2]],
            device_id=device, device_id_type=MESH)
        copy.start()
        sends.append(copy)

    def arrive(oz, ox, part):
        place = buf.at[lines(oz, ox), columns(part)]
        pltpu.make_async_copy(place, place, recv_sem.at[oz * X + ox, part[2]]).wait()

    def precondition_own(part):
        for i in range(part[1] // bsz):
            m = part[0] // bsz + i
            cols = columns((part[0] + i * bsz, bsz))
            first = jnp.dot(q[:, cols], basis[m], preferred_element_type=jnp.float32)
            rot[:, i * bsz:(i + 1) * bsz] = (first * inv[pl.ds(m, 1), :]).astype(jnp.bfloat16)
        for i in range(part[1] // bsz):
            m = part[0] // bsz + i
            second = lax.dot_general(rot[:, i * bsz:(i + 1) * bsz], basis[m], (((1,), (1,)), ((), ())),
                                     preferred_element_type=jnp.float32)
            buf[lines(z, x), columns((part[0] + i * bsz, bsz))] = second.astype(jnp.bfloat16)

    for load in loads[:3]:
        load.wait()
    precondition_own(mine)
    pl.semaphore_wait(barrier, Z + 2)
    for oz in planes:
        send(z, x, mine, {"blk": oz * X + x})
    precondition_own(other)
    send(z, x, whole, {"blk": z * X + 1 - x})

    def hand_over(oz):
        arrive(oz, 1 - x, mine)
        send(oz, 1 - x, mine, {"groups": 1 - y})

    for oz in planes:
        arrive(oz, x, mine)
        send(oz, x, mine, {"groups": 1 - y})
        send(oz, x, mine, {"blk": z * X + 1 - x})
    arrive(planes[0], x, other)
    send(planes[0], x, other, {"blk": z * X + 1 - x})
    for oz in planes[1:]:
        hand_over(oz)
    arrive(planes[0], 1 - x, mine)
    arrive(z, 1 - x, whole)

    def score(i, part):
        return lax.dot_general(buf[:, columns(part)], train[i, :, columns(part)], (((1,), (1,)), ((), ())),
                               preferred_element_type=jnp.float32)

    loads[3].wait()
    loads[4].wait()
    give[...] = score(1, mine)
    keep[...] = score(0, mine)
    for oz in planes:
        if oz is not planes[0]:
            arrive(oz, x, other)
        arrive(oz, 1 - x, other)
    give[...] += score(1, other)
    swap = pltpu.make_async_remote_copy(src_ref=give, dst_ref=got, send_sem=give_sem, recv_sem=got_sem,
                                        device_id={"dim": 1 - d}, device_id_type=MESH)
    swap.start()
    keep[...] += score(0, other)
    swap.wait_recv()
    out[...] = (keep[...] + got[...]) * (1.0 / (PROJ ** 0.5))
    for copy in sends:
        copy.wait_send()
    swap.wait_send()


def fused(queries, train_proj, basis, inv_eigen):
    rows, width = queries.shape
    examples = train_proj.shape[0]
    total = rows * X * Z
    half = (total, examples // 2)
    hbm = pl.BlockSpec(memory_space=pl.ANY)
    vmem = pl.BlockSpec(memory_space=pltpu.VMEM)
    return pl.pallas_call(
        kernel,
        out_shape=jax.ShapeDtypeStruct(half, jnp.float32),
        in_specs=[hbm] * 4,
        out_specs=vmem,
        scratch_shapes=[
            pltpu.VMEM((rows, width), jnp.bfloat16),
            pltpu.VMEM((rows, width), jnp.bfloat16),
            pltpu.VMEM((total, width), jnp.bfloat16),
            pltpu.VMEM((2, examples // 2, width), jnp.bfloat16),
            pltpu.VMEM(basis.shape, basis.dtype),
            pltpu.VMEM(inv_eigen.shape, inv_eigen.dtype),
            pltpu.VMEM(half, jnp.float32),
            pltpu.VMEM(half, jnp.float32),
            pltpu.VMEM(half, jnp.float32),
            pltpu.SemaphoreType.DMA((5,)),
            pltpu.SemaphoreType.DMA((4 * Z,)),
            pltpu.SemaphoreType.DMA((X * Z, 3)),
            pltpu.SemaphoreType.DMA,
            pltpu.SemaphoreType.DMA,
        ],
        compiler_params=pltpu.CompilerParams(
            collective_id=0, has_side_effects=True, vmem_limit_bytes=60 * 1024 * 1024),
        cost_estimate=pl.CostEstimate(flops=2 * total * width * (examples + 256), transcendentals=0,
                                      bytes_accessed=2 * width * (examples + 256)),
    )(queries, train_proj, basis, inv_eigen)


def precondition(queries, basis, inv_eigen):
    count = queries.shape[0]
    local_modules = basis.shape[0]
    width = basis.shape[1]
    blocks = queries.reshape(count, local_modules, width)
    rotated = (
        jnp.einsum("qmb,mbc->qmc", blocks, basis, preferred_element_type=jnp.float32)
        * inv_eigen[None, :, :]
    )
    rotated = rotated.astype(jnp.bfloat16)
    precond = jnp.einsum("qmc,mbc->qmb", rotated, basis, preferred_element_type=jnp.float32).astype(
        jnp.bfloat16
    )
    return precond.reshape(count, local_modules * width)


def shards(queries, train_proj, basis, inv_eigen):
    precond = precondition(queries, basis, inv_eigen)
    factor = 1.0 / jnp.sqrt(jnp.float32(PROJ))
    terms = lax.dot_general(
        lax.all_gather(precond, "blk", axis=0, tiled=True),
        train_proj,
        (((1,), (1,)), ((), ())),
        preferred_element_type=jnp.float32,
    )
    half = train_proj.shape[0] // lax.axis_size("dim")
    summed = lax.psum(terms, "dim")
    own = lax.dynamic_slice_in_dim(summed, lax.axis_index("dim") * half, half, 1)
    return own * factor


def solution(mesh):
    placed = (P("blk", "dim"), P(("groups", "blk"), "dim"), P("dim", None, None), P("dim", None))
    small = mesh.shape["blk"] == X * Z and mesh.shape["groups"] == 2 and mesh.shape["dim"] == 2
    return jax.shard_map(
        fused if small else shards,
        mesh=mesh,
        in_specs=placed,
        out_specs=P(None, ("groups", "blk", "dim")),
        check_vma=False,
    )
```

```python
import functools

import jax
import jax.numpy as jnp
from jax import lax
from jax.experimental import pallas as pl
from jax.experimental.pallas import tpu as pltpu
from jax.sharding import PartitionSpec as P

PROJ = 8192
MESH = pl.DeviceIdType.MESH
X = 2
Z = 4


def order(z, s):
    near = jnp.minimum(z, Z - 1 - z)
    both = s <= 2 * near
    side = jnp.where(both, 2 * (s % 2) - 1, jnp.where(2 * z < Z, 1, -1))
    dist = jnp.where(both, (s + 1) // 2, s - near)
    return z + side * dist, side


def kernel(q_hbm, train_hbm, basis_hbm, inv_hbm, out, q, rot, buf, train, basis, inv, keep, give, got,
           load_sem, send_sem, recv_sem, give_sem, got_sem):
    rows, width = q_hbm.shape
    half = train_hbm.shape[0] // 2
    bsz = basis_hbm.shape[1]
    y, b, d = lax.axis_index("groups"), lax.axis_index("blk"), lax.axis_index("dim")
    z, x = b // X, b % X
    planes = [order(z, s)[0] for s in range(1, Z)]

    barrier = pltpu.get_barrier_semaphore()

    def hello(**device):
        pl.semaphore_signal(barrier, inc=1, device_id=device, device_id_type=MESH)

    hello(blk=z * X + 1 - x)
    hello(groups=1 - y)
    hello(dim=1 - d)
    for oz in planes:
        hello(blk=oz * X + x)

    loads = [pltpu.make_async_copy(basis_hbm, basis, load_sem.at[0]),
             pltpu.make_async_copy(inv_hbm, inv, load_sem.at[1]),
             pltpu.make_async_copy(q_hbm, q, load_sem.at[2])]
    for i in range(2):
        at = pl.multiple_of((d if i == 0 else 1 - d) * half, 16)
        loads.append(pltpu.make_async_copy(train_hbm.at[pl.ds(at, half)], train.at[i], load_sem.at[3 + i]))
    for load in loads:
        load.start()

    split = width // 2
    mine = (y * split, split, y)
    other = ((1 - y) * split, split, 1 - y)
    whole = (0, width, 2)
    sends = []

    def columns(part):
        start = part[0] if isinstance(part[0], int) else pl.multiple_of(part[0], 128)
        return pl.ds(start, part[1])

    def lines(oz, ox):
        return pl.ds(pl.multiple_of((oz * X + ox) * rows, rows), rows)

    def send(oz, ox, part, device):
        place = buf.at[lines(oz, ox), columns(part)]
        copy = pltpu.make_async_remote_copy(
            src_ref=place, dst_ref=place,
            send_sem=send_sem.at[len(sends)], recv_sem=recv_sem.at[oz * X + ox, part[2]],
            device_id=device, device_id_type=MESH)
        copy.start()
        sends.append(copy)

    def arrive(oz, ox, part):
        place = buf.at[lines(oz, ox), columns(part)]
        pltpu.make_async_copy(place, place, recv_sem.at[oz * X + ox, part[2]]).wait()

    def precondition_own(part):
        for i in range(part[1] // bsz):
            m = part[0] // bsz + i
            cols = columns((part[0] + i * bsz, bsz))
            first = jnp.dot(q[:, cols], basis[m], preferred_element_type=jnp.float32)
            rot[:, i * bsz:(i + 1) * bsz] = (first * inv[pl.ds(m, 1), :]).astype(jnp.bfloat16)
        for i in range(part[1] // bsz):
            m = part[0] // bsz + i
            second = lax.dot_general(rot[:, i * bsz:(i + 1) * bsz], basis[m], (((1,), (1,)), ((), ())),
                                     preferred_element_type=jnp.float32)
            buf[lines(z, x), columns((part[0] + i * bsz, bsz))] = second.astype(jnp.bfloat16)

    for load in loads[:3]:
        load.wait()
    precondition_own(mine)
    pl.semaphore_wait(barrier, Z + 2)
    for oz in planes:
        send(z, x, mine, {"blk": oz * X + x})
    precondition_own(other)
    send(z, x, whole, {"blk": z * X + 1 - x})

    def hand_over(oz):
        arrive(oz, 1 - x, mine)
        send(oz, 1 - x, mine, {"groups": 1 - y})

    for oz in planes:
        arrive(oz, x, mine)
        send(oz, x, mine, {"groups": 1 - y})
        send(oz, x, mine, {"blk": z * X + 1 - x})
    arrive(planes[0], x, other)
    send(planes[0], x, other, {"blk": z * X + 1 - x})
    for oz in planes[1:]:
        hand_over(oz)
    arrive(planes[0], 1 - x, mine)
    arrive(z, 1 - x, whole)

    def score(i, part):
        return lax.dot_general(buf[:, columns(part)], train[i, :, columns(part)], (((1,), (1,)), ((), ())),
                               preferred_element_type=jnp.float32)

    loads[3].wait()
    loads[4].wait()
    give[...] = score(1, mine)
    keep[...] = score(0, mine)
    for oz in planes:
        if oz is not planes[0]:
            arrive(oz, x, other)
        arrive(oz, 1 - x, other)
    swaps = []
    count = give.shape[0] // 2
    for i in range(2):
        top = slice(i * count, (i + 1) * count)
        give[top, :] += lax.dot_general(buf[top, columns(other)], train[1, :, columns(other)],
                                        (((1,), (1,)), ((), ())), preferred_element_type=jnp.float32)
        here = pl.ds(i * count, count)
        swaps.append(pltpu.make_async_remote_copy(
            src_ref=give.at[here], dst_ref=got.at[here], send_sem=give_sem.at[i], recv_sem=got_sem.at[i],
            device_id={"dim": 1 - d}, device_id_type=MESH))
        swaps[i].start()
    keep[...] += score(0, other)
    for swap in swaps:
        swap.wait_recv()
    out[...] = (keep[...] + got[...]) * (1.0 / (PROJ ** 0.5))
    for copy in sends:
        copy.wait_send()
    for swap in swaps:
        swap.wait_send()


def fused(queries, train_proj, basis, inv_eigen):
    rows, width = queries.shape
    examples = train_proj.shape[0]
    total = rows * X * Z
    half = (total, examples // 2)
    hbm = pl.BlockSpec(memory_space=pl.ANY)
    vmem = pl.BlockSpec(memory_space=pltpu.VMEM)
    return pl.pallas_call(
        kernel,
        out_shape=jax.ShapeDtypeStruct(half, jnp.float32),
        in_specs=[hbm] * 4,
        out_specs=vmem,
        scratch_shapes=[
            pltpu.VMEM((rows, width), jnp.bfloat16),
            pltpu.VMEM((rows, width), jnp.bfloat16),
            pltpu.VMEM((total, width), jnp.bfloat16),
            pltpu.VMEM((2, examples // 2, width), jnp.bfloat16),
            pltpu.VMEM(basis.shape, basis.dtype),
            pltpu.VMEM(inv_eigen.shape, inv_eigen.dtype),
            pltpu.VMEM(half, jnp.float32),
            pltpu.VMEM(half, jnp.float32),
            pltpu.VMEM(half, jnp.float32),
            pltpu.SemaphoreType.DMA((5,)),
            pltpu.SemaphoreType.DMA((4 * Z,)),
            pltpu.SemaphoreType.DMA((X * Z, 3)),
            pltpu.SemaphoreType.DMA((2,)),
            pltpu.SemaphoreType.DMA((2,)),
        ],
        compiler_params=pltpu.CompilerParams(
            collective_id=0, has_side_effects=True, vmem_limit_bytes=60 * 1024 * 1024),
        cost_estimate=pl.CostEstimate(flops=2 * total * width * (examples + 256), transcendentals=0,
                                      bytes_accessed=2 * width * (examples + 256)),
    )(queries, train_proj, basis, inv_eigen)


def precondition(queries, basis, inv_eigen):
    count = queries.shape[0]
    local_modules = basis.shape[0]
    width = basis.shape[1]
    blocks = queries.reshape(count, local_modules, width)
    rotated = (
        jnp.einsum("qmb,mbc->qmc", blocks, basis, preferred_element_type=jnp.float32)
        * inv_eigen[None, :, :]
    )
    rotated = rotated.astype(jnp.bfloat16)
    precond = jnp.einsum("qmc,mbc->qmb", rotated, basis, preferred_element_type=jnp.float32).astype(
        jnp.bfloat16
    )
    return precond.reshape(count, local_modules * width)


def shards(queries, train_proj, basis, inv_eigen):
    precond = precondition(queries, basis, inv_eigen)
    factor = 1.0 / jnp.sqrt(jnp.float32(PROJ))
    terms = lax.dot_general(
        lax.all_gather(precond, "blk", axis=0, tiled=True),
        train_proj,
        (((1,), (1,)), ((), ())),
        preferred_element_type=jnp.float32,
    )
    half = train_proj.shape[0] // lax.axis_size("dim")
    summed = lax.psum(terms, "dim")
    own = lax.dynamic_slice_in_dim(summed, lax.axis_index("dim") * half, half, 1)
    return own * factor


def solution(mesh):
    placed = (P("blk", "dim"), P(("groups", "blk"), "dim"), P("dim", None, None), P("dim", None))
    small = mesh.shape["blk"] == X * Z and mesh.shape["groups"] == 2 and mesh.shape["dim"] == 2
    return jax.shard_map(
        fused if small else shards,
        mesh=mesh,
        in_specs=placed,
        out_specs=P(None, ("groups", "blk", "dim")),
        check_vma=False,
    )
```
